256 devices in a mesh: wide: 16 (over y, z_hi, core), expert: 16 (over z_lo, x).
Axes of the slice: x: 4, y: 4, z: 8 (z_hi: 2, z_lo: 4; z = z_hi * 4 + z_lo), core: 2. Of those that a mesh axis runs over, the one named last changes fastest.
Arguments:
- prompt: bfloat16 [2048, 4096], P('expert'), may hold values from -6 to 6
- steer_vec: float32 [4096], replicated, may hold values from -6 to 6
- strengths: float32 [16], P('wide'), may hold values from -2 to 2
- norm_gain: float32 [4096], replicated, may hold values from 0.25 to 1.75
- expert_ids: int32 [2048, 8], P('expert'), may hold values from 0 to 15, all different within a row; in each aligned block of 128 rows (0 to 127, 128 to 255, ...) at most 72 rows name the same one
- gate_values: float32 [2048, 8], P('expert'), may hold values from 0.02 to 0.5
- up_weight: bfloat16 [16, 4096, 768], P('expert', 'wide'), may hold values from -0.09375 to 0.09375
- down_weight: bfloat16 [16, 768, 4096], P('expert', None, 'wide'), may hold values from -0.21875 to 0.21875
Outputs:
- mixed: bfloat16 [16, 2048, 4096], P('wide', 'expert')
The draws below stay inside these ranges and needn't reach their ends.
Inputs may be any that keep to these rules, and one draw needn't show every extreme that they name: `expert_ids`: each row names 8 different experts. Among the rows of one device of expert (aligned blocks of 128 rows) no expert is named more than 72 times, and in every draw some expert is named exactly 72 times in some block.
All inputs are finite; a program needn't handle non-finite values.
Results may differ from the reference program's by a relative error of at most 0.0065.
Values may be sent and summed in bfloat16 or wider, within the bound.
A program may use at most 128 MiB of HBM per device.

```python
import math
import jax
import jax.numpy as jnp
import numpy as np
from jax import lax

D = 4096
EH = 768
TOP = 8
TOK_DEV = 128
EXPERTS = 16
STRENGTHS = 16
GROUP = 2048
CAP = 72
N_EXPERT = 16


def levels(stream_key, dims, shards, least, largest):
    factor_of = 1.0
    for position, blocks in shards:
        heights = jax.random.uniform(jax.random.fold_in(jax.random.fold_in(stream_key, 6), position), (blocks,), jnp.float32, least / len(shards), largest / len(shards))
        factor_of = factor_of * jnp.repeat(jnp.exp(heights), dims[position] // blocks).reshape((-1,) + (1,) * (len(dims) - 1 - position))
    return factor_of


def deal_out(own_key, own, number, rows, number_of, top, reach, slope):
    sequence = jax.random.permutation(own_key, number_of)
    packed, ordinary = portions_of(number_of, rows * top, reach, slope, True), portions_of(number_of, rows * top, reach, slope, False)
    places = jnp.arange(number_of)

    def named(sizes, rotation):
        used = int((sizes > 0).sum())
        fixed = max(1, used // 4)
        moved = fixed + (places - fixed + rotation * (used - fixed)) % max(1, number_of - fixed)
        return jnp.zeros((number_of,), jnp.int32).at[sequence[jnp.where(places < fixed, places, moved)]].set(jnp.asarray(sizes, jnp.int32))

    sizes = jnp.where(number % 4 == 0, named(packed, number // 4), named(ordinary, number - number // 4 - 1))
    mixed = jax.random.permutation(jax.random.fold_in(own, 3), number_of)
    donor, receiver = mixed[0:number_of // 2 * 2:2], mixed[1:number_of // 2 * 2:2]
    slack = jnp.minimum(sizes[donor] - 1, reach - sizes[receiver]) // 2
    slack = jnp.where((donor == sequence[0]) | (receiver == sequence[0]) | (sizes[receiver] == 0), 0, jnp.maximum(slack, 0))
    moved = jax.random.randint(jax.random.fold_in(own, 4), (number_of // 2,), 0, 1 << 20) % (slack + 1)
    sizes = sizes.at[donor].add(-moved).at[receiver].add(moved)
    items = jnp.searchsorted(jnp.cumsum(sizes), jnp.arange(rows * top), side="right").astype(jnp.int32)
    table = items.reshape(top, rows).T
    table = table[jax.random.permutation(jax.random.fold_in(own, 1), rows)]
    rotation = jax.random.randint(jax.random.fold_in(own, 2), (rows, 1), 0, top)
    return jnp.take_along_axis(table, (jnp.arange(top)[None, :] + rotation) % top, axis=1)


def portions_of(count, total, bound, lean, full):
    portions = [(1 << 20) // math.isqrt(standing ** lean) + 1 for standing in range(1, count + 1)]
    largest = bound if full else min(bound, max(-(-total // count), total * portions[0] // sum(portions)))
    least = 1 if total - largest >= count - 1 else 0
    holding, surplus = [largest] + [least] * (count - 1), total - largest - least * (count - 1)
    while surplus > 0:
        candidates = [i for i in range(1, count) if holding[i] < largest] or [i for i in range(1, count) if holding[i] < bound]
        pool, remaining = sum([portions[i] for i in candidates]), surplus
        for i in candidates:
            extra = min(bound - holding[i], max(1, remaining * portions[i] // pool), surplus)
            holding[i] = holding[i] + extra
            surplus = surplus - extra
    return np.array(holding)


def centred(own_key, dims, deviation, reach, split=(), held_as=jnp.bfloat16):
    loudness = levels(own_key, dims, split, -0.22, 0.18) if split else 1.0
    values = jax.random.normal(own_key, dims, jnp.float32) * deviation * loudness
    return jnp.minimum(jnp.maximum(values, -reach), reach).astype(held_as)


def setup_inputs(seed: int = 0) -> dict:
    streams_of = jax.random.split(jax.random.key(seed), 9)
    prompt = centred(streams_of[0], (GROUP, D), 1.0, 6.0, ((0, 16),))
    steer_vec = centred(streams_of[1], (D,), 1.0, 6.0, (), jnp.float32)
    strengths = jnp.clip(jax.random.uniform(streams_of[2], (STRENGTHS,), jnp.float32, -2.0, 2.0) * levels(streams_of[2], (STRENGTHS,), ((0, 16),), -0.4, 0.0), -2.0, 2.0)
    norm_gain = jnp.clip(1.0 + 0.15 * jax.random.normal(streams_of[3], (D,), jnp.float32), 0.25, 1.75)
    expert_ids_keys = jax.random.split(jax.random.fold_in(streams_of[4], 1), GROUP // TOK_DEV)
    expert_ids_turns = jax.random.permutation(jax.random.fold_in(streams_of[4], 3), GROUP // TOK_DEV)
    expert_ids = jax.vmap(lambda own, number: deal_out(jax.random.fold_in(streams_of[4], 2), own, number, TOK_DEV, EXPERTS, TOP, CAP, 1))(expert_ids_keys, expert_ids_turns).reshape((GROUP, TOP))
    gate_values = jnp.clip(jnp.exp(math.log(0.5) - 3.218876 * jax.random.uniform(streams_of[5], (GROUP, TOP), jnp.float32) ** levels(streams_of[5], (GROUP, TOP), ((0, 16),), -0.2, 0.2)), 0.02, 0.5)
    up_weight = centred(streams_of[6], (EXPERTS, D, EH), D ** -0.5, 0.09375, ((0, 16), (1, 16)))
    down_weight = centred(streams_of[7], (EXPERTS, EH, D), EH ** -0.5, 0.21875, ((0, 16), (2, 16)))
    return dict(prompt=prompt, steer_vec=steer_vec, strengths=strengths, norm_gain=norm_gain, expert_ids=expert_ids, gate_values=gate_values, up_weight=up_weight, down_weight=down_weight)


epsilon = 1e-06

def steer_rows(rows, strength, steer_vec, norm_gain):
    shifted = rows.astype(jnp.float32) + strength * steer_vec
    mean_square = lax.optimization_barrier(jnp.mean(shifted * shifted, axis=-1, keepdims=True))
    return (shifted * lax.rsqrt(mean_square + epsilon) * norm_gain).astype(jnp.bfloat16)

def slot_numbers(expert_ids):
    blocks = expert_ids.reshape(N_EXPERT, TOK_DEV * TOP)
    onehot = (blocks[:, :, None] == jnp.arange(EXPERTS, dtype=jnp.int32)[None, None, :]).astype(jnp.int32)
    earlier = jnp.cumsum(onehot, axis=1) - onehot
    return lax.optimization_barrier(jnp.sum(earlier * onehot, axis=2)).reshape(GROUP, TOP)

def reference(prompt, steer_vec, strengths, norm_gain, expert_ids, gate_values, up_weight, down_weight):
    slots = slot_numbers(expert_ids)
    source = (jnp.arange(GROUP, dtype=jnp.int32) // TOK_DEV)[:, None]
    positions = (source * CAP + slots).astype(jnp.int32)
    total_rows = N_EXPERT * CAP
    token_index = jnp.broadcast_to(jnp.arange(GROUP, dtype=jnp.int32)[:, None], (GROUP, TOP))

    def per_strength(strength):
        normed = steer_rows(prompt, strength, steer_vec, norm_gain)

        def per_expert(expert_index, total):
            chosen = expert_ids == expert_index
            target = jnp.where(chosen, positions, total_rows).reshape(-1)
            table = jnp.zeros((total_rows,), jnp.int32).at[target].set(token_index.reshape(-1), mode='drop')
            gathered = normed[table].astype(jnp.float32)
            upper = up_weight[expert_index].astype(jnp.float32)
            lower = down_weight[expert_index].astype(jnp.float32)
            hidden = jax.nn.silu(jnp.dot(gathered, upper, precision=lax.Precision.HIGHEST)).astype(jnp.bfloat16)
            outputs = jnp.dot(hidden.astype(jnp.float32), lower, precision=lax.Precision.HIGHEST).astype(jnp.bfloat16)
            weight = lax.optimization_barrier(jnp.sum(jnp.where(chosen, gate_values, 0.0), axis=1))
            where_row = lax.optimization_barrier(jnp.sum(jnp.where(chosen, positions, 0), axis=1)).astype(jnp.int32)
            return total + weight[:, None] * outputs[where_row].astype(jnp.float32)
        summed = lax.fori_loop(0, EXPERTS, per_expert, jnp.zeros((GROUP, D), jnp.float32))
        return summed.astype(jnp.bfloat16)
    return lax.map(per_strength, strengths)
```

```python
import jax
import jax.numpy as jnp
from jax import lax
from jax.sharding import Mesh, PartitionSpec as P

D = 4096
EH = 768
epsilon = 1e-06

WIDE = ("y", "zh", "c")
EXPERT = ("zl", "x")


def local(prompt, steer_vec, strengths, norm_gain, expert_ids, gate_values, up_weight, down_weight):
    w = lax.axis_index(WIDE)
    x = lax.axis_index("x")
    rows = prompt.astype(jnp.float32)
    scaled = (rows * norm_gain).astype(jnp.bfloat16)
    part = lax.dynamic_slice(scaled, (0, w * 256), (128, 256))
    part = lax.all_gather(part, EXPERT, axis=0, tiled=True)
    upper = jnp.dot(part, up_weight[0], preferred_element_type=jnp.float32)
    upper = upper.astype(jnp.bfloat16).reshape(4, 4, 16, 8, EH).transpose(2, 0, 1, 3, 4)
    upper = lax.all_to_all(upper, WIDE, split_axis=0, concat_axis=0, tiled=True)
    upper = jnp.sum(upper.astype(jnp.float32), axis=0).astype(jnp.bfloat16)
    upper = lax.all_to_all(upper, "zl", split_axis=0, concat_axis=0, tiled=True)
    upper = lax.all_gather(upper, WIDE, axis=0)
    upper = upper.transpose(1, 2, 0, 3, 4).reshape(4, 512, EH)

    steer = lax.dynamic_slice(steer_vec * norm_gain, (w * 256,), (256,))
    high = steer.astype(jnp.bfloat16)
    low = (steer - high.astype(jnp.float32)).astype(jnp.bfloat16)
    push = jnp.dot(jnp.stack([high, low]), up_weight[0], preferred_element_type=jnp.float32)
    push = lax.psum(jnp.sum(push, axis=0), WIDE)
    push = lax.all_gather(push, "zl", axis=0)

    s4 = lax.all_gather(strengths[0], "y", axis=0)
    shifted = rows[None] + s4[:, None, None] * steer_vec
    inv = lax.rsqrt(jnp.mean(shifted * shifted, axis=-1) + epsilon)
    inv = lax.all_gather(inv, "x", axis=1, tiled=True)

    onehot = expert_ids[:, :, None] == jnp.arange(16, dtype=jnp.int32)
    gates = jnp.sum(jnp.where(onehot, gate_values[:, :, None], 0.0), axis=1)
    gates = lax.all_gather(gates, "x", axis=0, tiled=True).reshape(512, 4, 4)
    gates = lax.dynamic_index_in_dim(gates, x, axis=2, keepdims=False).T

    lower = lax.all_gather(down_weight[0], ("zh", "c", "zl"), axis=0)
    lower = lower.reshape(4, 4, EH, 256).transpose(1, 2, 0, 3).reshape(4 * EH, 1024)

    pre = upper[None].astype(jnp.float32) + s4[:, None, None, None] * push[None, :, None, :]
    hidden = jax.nn.silu(pre * inv[:, None, :, None]) * gates[None, :, :, None]
    hidden = hidden.astype(jnp.bfloat16).transpose(0, 2, 1, 3).reshape(4 * 512, 4 * EH)
    out = jnp.dot(hidden, lower, preferred_element_type=jnp.float32).astype(jnp.bfloat16)
    out = out.reshape(16, 128, 1024)
    out = lax.all_to_all(out, ("y", "x"), split_axis=0, concat_axis=0, tiled=True)
    out = jnp.sum(out.reshape(4, 4, 128, 1024).astype(jnp.float32), axis=1)
    return out.transpose(1, 0, 2).reshape(1, 128, D).astype(jnp.bfloat16)


def solution(mesh):
    fine = Mesh(mesh.devices.reshape(4, 2, 2, 4, 4), ("y", "zh", "c", "zl", "x"))
    return jax.shard_map(
        local,
        mesh=fine,
        in_specs=(
            P(EXPERT, None),
            P(),
            P(WIDE),
            P(),
            P(EXPERT, None),
            P(EXPERT, None),
            P(EXPERT, WIDE, None),
            P(EXPERT, None, WIDE),
        ),
        out_specs=P(WIDE, EXPERT, None),
        check_vma=False,
    )
```

```python
import jax
import jax.numpy as jnp
from jax import lax
from jax.experimental import pallas as pl
from jax.experimental.pallas import tpu as pltpu
from jax.sharding import Mesh, PartitionSpec as P

D = 4096
EH = 768
epsilon = 1e-06

WIDE = ("y", "zh", "c")
EXPERT = ("zl", "x")
MESH = pl.DeviceIdType.MESH
F32 = jnp.float32
BF16 = jnp.bfloat16
TURN = (2, 1, 3, 0)


def kernel(
    prompt, steer, strength, gain, ids, gates, up, down, out,
    sbuf, pgb, misc, ub, db, psend, precv, upper, aown, ab, qb, hb, part, rsend, rrecv, msend, mrecv, fin,
    load_sem, s_snd, s_rcv, p_snd, p_rcv, m_snd, m_rcv, ring_snd, ring_rcv, sib_snd, sib_rcv,
    rs_snd, rs_rcv, ag_snd, ag_rcv, q_snd, q_rcv, rl_snd, rl_rcv, mn_snd, mn_rcv, f_snd, f_rcv, f_loc,
):
    y, zh, c = lax.axis_index("y"), lax.axis_index("zh"), lax.axis_index("c")
    zl, x = lax.axis_index("zl"), lax.axis_index("x")
    zz = zh * 4 + zl
    sib = 1 - c

    def at_z(step):
        z = lax.rem(zz + step + 8, 8)
        return z // 4, lax.rem(z, 4)

    def z_id(step):
        a, b = at_z(step)
        return {"zh": a, "zl": b}

    def x_id(d):
        return {"x": lax.rem(x + d, 4)}

    def yc_id(d, b):
        return {"y": lax.rem(y + d, 4), "c": lax.rem(c + b, 2)}

    def remote(src, dst, snd, rcv, dev):
        return pltpu.make_async_remote_copy(
            src_ref=src, dst_ref=dst, send_sem=snd, recv_sem=rcv, device_id=dev, device_id_type=MESH
        )

    def slot(t, step, core, half=None):
        a, b = at_z(step)
        if t == 0:
            if half is None:
                return ub.at[b, pl.ds((a * 2 + core) * 256, 256), :]
            return ub.at[b, pl.ds((a * 2 + core) * 256 + half * 128, 128), :]
        if half is None:
            return db.at[a, core, pl.ds(b * EH, EH), :]
        return db.at[a, core, pl.ds(b * EH + half * 384, 384), :]

    load = [
        pltpu.make_async_copy(up, slot(0, 0, c), load_sem.at[0]),
        pltpu.make_async_copy(down, slot(1, 0, c), load_sem.at[1]),
    ]
    for cp in load:
        cp.start()

    partners = [z_id(1), z_id(-1)] + [x_id(d) for d in (1, 2, 3)]
    partners += [yc_id(d, b) for d in range(4) for b in range(2) if d or b]
    barrier = pltpu.get_barrier_semaphore()
    for dev in partners:
        pl.semaphore_signal(barrier, inc=1, device_id=dev, device_id_type=MESH)
    pl.semaphore_wait(barrier, len(partners))

    def ring(t, way, k):
        sign = 1 if way == 0 else -1
        half = way if k == 4 else None
        piece = slot(t, -sign * (k - 1), c, half)
        return remote(piece, piece, ring_snd.at[t, way, k - 1], ring_rcv.at[t, way, k - 1], z_id(sign))

    def ring_send(t, k):
        for way in (0, 1):
            ring(t, way, k).start()

    def sibling(t, n):
        step = (0, -1, 1, -2, 2, -3, 3, 4)[n]
        piece = slot(t, step, c)
        return remote(piece, piece, sib_snd.at[t, n], sib_rcv.at[t, n], {"c": sib})

    def ring_take(t, k):
        for way in (0, 1):
            ring(t, way, k).wait_recv()
        if k < 4:
            ring_send(t, k + 1)
            sibling(t, 2 * k - 1).start()
            sibling(t, 2 * k).start()
        else:
            sibling(t, 7).start()

    load[0].wait()
    ring_send(0, 1)
    sibling(0, 0).start()

    me = y * 2 + c
    sbuf[me] = strength[...]
    others = [(d, b) for d in range(4) for b in range(2) if d or b]

    def strengths_copy(d, b):
        n = d * 2 + b
        return remote(sbuf.at[me], sbuf.at[me], s_snd.at[n], s_rcv.at[n], yc_id(d, b))

    for d, b in others:
        strengths_copy(d, b).start()

    rows = pl.ds(pl.multiple_of(c * 64, 64), 64)
    cols = pl.ds(pl.multiple_of(y * 1024, 1024), 1024)
    mine = pl.ds(pl.multiple_of(x * 64, 64), 64)
    pgb[mine, :] = (prompt[rows, cols].astype(F32) * gain[:, cols]).astype(BF16)

    def prompt_copy(d):
        return remote(pgb.at[mine, :], pgb.at[mine, :], p_snd.at[d], p_rcv.at[d], x_id(d))

    for d in (1, 2, 3):
        prompt_copy(d).start()
    steered = steer[:, cols] * gain[:, cols]
    high = steered.astype(BF16).astype(F32)
    which = lax.broadcasted_iota(jnp.int32, (16, 1024), 0)
    pgb[256:272, :] = jnp.where(which == 0, high, jnp.where(which == 1, steered - high, 0.0)).astype(BF16)

    load[1].wait()
    sibling(1, 0).start()
    ring_take(0, 1)

    for d, b in others:
        strengths_copy(d, b).wait()
    lane = lax.broadcasted_iota(jnp.int32, (64, 128), 1)
    table = jnp.zeros((64, 128), F32)
    for k in range(8):
        table = table + jnp.where(lane == ids[rows, k:k + 1], gates[rows, k:k + 1], 0.0)
    misc[x] = table

    @pl.loop(0, 8)
    def _(j):
        s = sbuf[j][0:1, 0:1]
        square = jnp.zeros((64, 1), F32)
        for n in range(8):
            piece = prompt[rows, n * 512:(n + 1) * 512].astype(F32) + s * steer[:, n * 512:(n + 1) * 512]
            square = square + jnp.sum(piece * piece, axis=1, keepdims=True)
        misc[x] = misc[x] + jnp.where(lane == 16 + j, lax.rsqrt(square * (1.0 / D) + epsilon), 0.0)

    def misc_copy(d):
        return remote(misc.at[x], misc.at[x], m_snd.at[d], m_rcv.at[d], x_id(d))

    for d in (1, 2, 3):
        misc_copy(d).start()

    def turn(i):
        return lax.rem(zl + TURN[i], 4)

    def scatter_copy(i, d):
        e = turn(i)
        return remote(
            psend.at[e, lax.rem(y + d, 4)], precv.at[e, y], rs_snd.at[i, d], rs_rcv.at[i, d], yc_id(d, 0)
        )

    def expert(i):
        for n in ((3, 4), (2, 5), (1, 6), (0, 7))[i]:
            sibling(0, n).wait_recv()
        e = turn(i)
        for n in range(3):
            third = slice(n * 256, (n + 1) * 256)
            upper[...] = jnp.dot(pgb[...], ub[e, :, third], preferred_element_type=F32)
            for block in range(4):
                psend[e, block, :, third] = upper[block * 64:(block + 1) * 64, :].astype(BF16)
            aown[e, :, third] = upper[pl.ds(pl.multiple_of(y * 64, 64), 64), :]
            push = upper[256:264, :]
            qb[y, e, :, third] = push[0:1] + push[1:2] + jnp.zeros((8, 256), F32)
        for d in (1, 2, 3):
            scatter_copy(i, d).start()

    def gather_copy(i, d):
        e = turn(i)
        return remote(ab.at[y, e], ab.at[y, e], ag_snd.at[i, d], ag_rcv.at[i, d], yc_id(d, 0))

    def add_up(i):
        e = turn(i)
        total = aown[e]
        for d in (1, 2, 3):
            scatter_copy(i, d).wait_recv()
            total = total + precv[e, lax.rem(y + 4 - d, 4)].astype(F32)
        ab[y, e] = total.astype(BF16)
        for d in (1, 2, 3):
            gather_copy(i, d).start()

    def push_copy(d):
        return remote(qb.at[y], qb.at[y], q_snd.at[d], q_rcv.at[d], yc_id(d, 0))

    ring_take(0, 2)
    for d in (1, 2, 3):
        prompt_copy(d).wait_recv()
    expert(0)
    ring_take(0, 3)
    ring_send(1, 1)
    expert(1)
    expert(2)
    add_up(0)
    ring_take(0, 4)
    expert(3)
    for d in (1, 2, 3):
        push_copy(d).start()
    ring_take(1, 1)
    add_up(1)
    add_up(2)
    add_up(3)
    for d in (1, 2, 3):
        push_copy(d).wait_recv()
        misc_copy(d).wait_recv()
    for i in range(4):
        for d in (1, 2, 3):
            gather_copy(i, d).wait_recv()

    def hidden(g):
        dest_y = lax.rem(y + g + 1, 4)

        @pl.loop(0, 16)
        def _(n):
            block, e = n // 4, lax.rem(n, 4)
            pre = ab[block, e].astype(F32)
            here = misc[block]
            gate = jnp.sum(jnp.where(lane == e * 4 + x, here, 0.0), axis=1, keepdims=True)
            push = qb[0, e][0:1] + qb[1, e][0:1] + qb[2, e][0:1] + qb[3, e][0:1]
            for b in range(2):
                j = dest_y * 2 + b
                inv = 0.5 * jnp.sum(jnp.where(lane == 16 + j, here, 0.0), axis=1, keepdims=True)
                half = (pre + sbuf[j][0:1, 0:1] * push) * inv
                value = (half * gate) * (1.0 + jnp.tanh(half))
                hb[g, pl.ds(pl.multiple_of(block * 128 + b * 64, 64), 64),
                   pl.ds(pl.multiple_of(e * EH, 128), EH)] = value.astype(BF16)

    for k in (2, 3, 4):
        hidden(k - 2)
        ring_take(1, k)
    hidden(3)
    for n in range(8):
        sibling(1, n).wait_recv()

    def relay(g, way):
        return remote(
            rsend.at[g, way], rrecv.at[g, way], rl_snd.at[g, way], rl_rcv.at[g, way], x_id(1 + 2 * way)
        )

    def main(g, way):
        return remote(
            msend.at[g, way], mrecv.at[g, way], mn_snd.at[g, way], mn_rcv.at[g, way], x_id(1 + 2 * way)
        )

    def final(g, b):
        return remote(
            fin.at[g, pl.ds(pl.multiple_of(lax.rem(c + b, 2) * 64, 64), 64), :],
            out.at[0, rows, cols], f_snd.at[g, b], f_rcv.at[g, b], yc_id(g + 1, b),
        )

    def final_local():
        return pltpu.make_async_copy(fin.at[3, rows, :], out.at[0, rows, cols], f_loc)

    @pl.loop(0, 6)
    def _(t):
        @pl.when(t < 4)
        def _():
            @pl.loop(0, 2)
            def _(way):
                @pl.loop(0, 2)
                def _(n):
                    sums = jnp.dot(hb[t], db[way, n], preferred_element_type=F32)
                    place = pl.ds(pl.multiple_of(way * 512 + n * 256, 256), 256)
                    for block in range(4):
                        part[t, block, :, place] = sums[block * 128:(block + 1) * 128]
                    rsend[t, way, :, pl.ds(pl.multiple_of(n * 256, 256), 256)] = (
                        part[t, lax.rem(x + 2, 4), :, place].astype(BF16)
                    )

                relay(t, way).start()

        @pl.when(jnp.logical_and(t >= 1, t < 5))
        def _():
            g = t - 1
            for way in (0, 1):
                relay(g, way).wait_recv()
                block = lax.rem(x + 1 + 2 * way, 4)
                same = slice(way * 512, way * 512 + 512)
                other = slice(512 - way * 512, 1024 - way * 512)
                msend[g, way, :, same] = (part[g, block, :, same] + rrecv[g, way].astype(F32)).astype(BF16)
                msend[g, way, :, other] = part[g, block, :, other].astype(BF16)
                main(g, way).start()

        @pl.when(t >= 2)
        def _():
            g = t - 2
            main(g, 0).wait_recv()
            main(g, 1).wait_recv()
            fin[g] = (part[g, x] + mrecv[g, 0].astype(F32) + mrecv[g, 1].astype(F32)).astype(BF16)
            final(g, 1).start()

            @pl.when(g < 3)
            def _():
                final(g, 0).start()

            @pl.when(g == 3)
            def _():
                final_local().start()

    for d in (1, 2, 3):
        prompt_copy(d).wait_send()
        misc_copy(d).wait_send()
        push_copy(d).wait_send()
        for i in range(4):
            scatter_copy(i, d).wait_send()
            gather_copy(i, d).wait_send()
    for t in (0, 1):
        for k in (1, 2, 3, 4):
            for way in (0, 1):
                ring(t, way, k).wait_send()
        for n in range(8):
            sibling(t, n).wait_send()
    for g in range(4):
        for way in (0, 1):
            relay(g, way).wait_send()
            main(g, way).wait_send()
            if (g, way) != (3, 0):
                final(g, way).wait()
    final_local().wait()


def local(prompt, steer_vec, strengths, norm_gain, expert_ids, gate_values, up_weight, down_weight):
    vmem = pl.BlockSpec(memory_space=pltpu.VMEM)
    away = pl.BlockSpec(memory_space=pl.ANY)
    dma = pltpu.SemaphoreType.DMA
    return pl.pallas_call(
        kernel,
        out_shape=jax.ShapeDtypeStruct((1, 128, D), BF16),
        in_specs=[vmem] * 6 + [away] * 2,
        out_specs=away,
        scratch_shapes=[
            pltpu.VMEM((8, 8, 128), F32),
            pltpu.VMEM((272, 1024), BF16),
            pltpu.VMEM((4, 64, 128), F32),
            pltpu.VMEM((4, 1024, EH), BF16),
            pltpu.VMEM((2, 2, 4 * EH, 256), BF16),
            pltpu.VMEM((4, 4, 64, EH), BF16),
            pltpu.VMEM((4, 4, 64, EH), BF16),
            pltpu.VMEM((272, 256), F32),
            pltpu.VMEM((4, 64, EH), F32),
            pltpu.VMEM((4, 4, 64, EH), BF16),
            pltpu.VMEM((4, 4, 8, EH), F32),
            pltpu.VMEM((4, 512, 4 * EH), BF16),
            pltpu.VMEM((4, 4, 128, 1024), F32),
            pltpu.VMEM((4, 2, 128, 512), BF16),
            pltpu.VMEM((4, 2, 128, 512), BF16),
            pltpu.VMEM((4, 2, 128, 1024), BF16),
            pltpu.VMEM((4, 2, 128, 1024), BF16),
            pltpu.VMEM((4, 128, 1024), BF16),
            dma((2,)),
            dma((8,)), dma((8,)),
            dma((4,)), dma((4,)),
            dma((4,)), dma((4,)),
            dma((2, 2, 4)), dma((2, 2, 4)),
            dma((2, 8)), dma((2, 8)),
            dma((4, 4)), dma((4, 4)),
            dma((4, 4)), dma((4, 4)),
            dma((4,)), dma((4,)),
            dma((4, 2)), dma((4, 2)),
            dma((4, 2)), dma((4, 2)),
            dma((4, 2)), dma((4, 2)),
            dma(()),
        ],
        compiler_params=pltpu.CompilerParams(
            collective_id=0, has_side_effects=True, vmem_limit_bytes=60 * 1024 * 1024
        ),
        cost_estimate=pl.CostEstimate(flops=18_000_000_000, bytes_accessed=3_000_000, transcendentals=6_300_000),
    )(
        prompt,
        steer_vec[None],
        jnp.broadcast_to(strengths, (8, 128)),
        norm_gain[None],
        expert_ids,
        gate_values,
        up_weight[0],
        down_weight[0],
    )


def solution(mesh):
    fine = Mesh(mesh.devices.reshape(4, 2, 2, 4, 4), ("y", "zh", "c", "zl", "x"))
    return jax.shard_map(
        local,
        mesh=fine,
        in_specs=(
            P(EXPERT, None),
            P(),
            P(WIDE),
            P(),
            P(EXPERT, None),
            P(EXPERT, None),
            P(EXPERT, WIDE, None),
            P(EXPERT, None, WIDE),
        ),
        out_specs=P(WIDE, EXPERT, None),
        check_vma=False,
    )
```

```python
import jax
import jax.numpy as jnp
from jax import lax
from jax.experimental import pallas as pl
from jax.experimental.pallas import tpu as pltpu
from jax.sharding import Mesh, PartitionSpec as P

D = 4096
EH = 768
epsilon = 1e-06

WIDE = ("y", "zh", "c")
EXPERT = ("zl", "x")
MESH = pl.DeviceIdType.MESH
F32 = jnp.float32
BF16 = jnp.bfloat16
TURN = (2, 1, 3, 0)


def kernel(
    prompt, steer, strength, gain, ids, gates, up, down, out,
    sbuf, by_row, pgb, misc, gt, it, sq, ub, db, ab, qb, hb, part, rsend, rrecv, msend, mrecv, fin,
    load_sem, s_snd, s_rcv, p_snd, p_rcv, m_snd, m_rcv, ring_snd, ring_rcv, sib_snd, sib_rcv,
    a_snd, a_rcv, a_loc, ag_snd, ag_rcv, q_snd, q_rcv, rl_snd, rl_rcv, mn_snd, mn_rcv, f_snd, f_rcv, f_loc,
):
    y, zh, c = lax.axis_index("y"), lax.axis_index("zh"), lax.axis_index("c")
    zl, x = lax.axis_index("zl"), lax.axis_index("x")
    zz = zh * 4 + zl
    sib = 1 - c

    def at_z(step):
        z = lax.rem(zz + step + 8, 8)
        return z // 4, lax.rem(z, 4)

    def z_id(step):
        a, b = at_z(step)
        return {"zh": a, "zl": b}

    def x_id(d):
        return {"x": lax.rem(x + d, 4)}

    def yc_id(d, b):
        return {"y": lax.rem(y + d, 4), "c": lax.rem(c + b, 2)}

    def remote(src, dst, snd, rcv, dev):
        return pltpu.make_async_remote_copy(
            src_ref=src, dst_ref=dst, send_sem=snd, recv_sem=rcv, device_id=dev, device_id_type=MESH
        )

    def column(at_y, e):
        return lax.rem(at_y - e + 8, 4)

    def slot(p, step, core, h):
        a, b = at_z(step)
        if p == 0:
            return ub.at[b, pl.ds(2 * h, 2), a, core]
        return db.at[p - 1, a, pl.ds(pl.multiple_of(b * EH + h * 384, 128), 384),
                     pl.ds(pl.multiple_of(core * 128, 128), 128)]

    def held(p, step, fn):
        if p:
            fn()
        else:
            pl.when(column(y, at_z(step)[1]) < 3)(fn)

    load = [None]
    for p in (0, 1):
        load.append(pltpu.make_async_copy(
            down.at[:, p * 128:(p + 1) * 128],
            db.at[p, zh, pl.ds(pl.multiple_of(zl * EH, 128), EH), pl.ds(pl.multiple_of(c * 128, 128), 128)],
            load_sem.at[1 + p],
        ))
    for cp in load[1:]:
        cp.start()

    partners = [z_id(1), z_id(-1)] + [x_id(d) for d in (1, 2, 3)]
    partners += [yc_id(d, b) for d in range(4) for b in range(2) if d or b]
    barrier = pltpu.get_barrier_semaphore()
    for dev in partners:
        pl.semaphore_signal(barrier, inc=1, device_id=dev, device_id_type=MESH)
    pl.semaphore_wait(barrier, len(partners))

    def ring(p, h, way, k):
        sign = 1 if way == 0 else -1
        piece = slot(p, -sign * (k - 1), c, h)
        return remote(piece, piece, ring_snd.at[p, h, way, k - 1], ring_rcv.at[p, h, way, k - 1], z_id(sign))

    def ways(h, k):
        return (0, 1) if k < 4 else (h,)

    def ring_send(p, h, k):
        for way in ways(h, k):
            held(p, (k - 1) * (2 * way - 1), ring(p, h, way, k).start)

    def sibling_step(n):
        return (0, -1, 1, -2, 2, -3, 3, 4)[n]

    def sibling(p, h, n):
        piece = slot(p, sibling_step(n), c, h)
        return remote(piece, piece, sib_snd.at[p, h, n], sib_rcv.at[p, h, n], {"c": sib})

    def sibling_send(p, h, n):
        held(p, sibling_step(n), sibling(p, h, n).start)

    def ring_take(p, k):
        for h in (0, 1):
            for way in ways(h, k):
                held(p, k * (2 * way - 1), ring(p, h, way, k).wait_recv)
            if k < 4:
                ring_send(p, h, k + 1)
                sibling_send(p, h, 2 * k - 1)
                sibling_send(p, h, 2 * k)
            else:
                sibling_send(p, h, 7)

    def columns_copy(d):
        b = lax.rem(column(y + d, zl), 3)
        return remote(
            up.at[:, pl.ds(pl.multiple_of(b * 256, 256), 256)], ub.at[zl, y, zh, c],
            a_snd.at[d], a_rcv.at[d], yc_id(d, 0),
        )

    def columns_own():
        b = lax.rem(column(y, zl), 3)
        return pltpu.make_async_copy(
            up.at[:, pl.ds(pl.multiple_of(b * 256, 256), 256)], ub.at[zl, y, zh, c], a_loc
        )

    held(0, 0, columns_own().start)
    for d in (1, 2, 3):
        pl.when(column(y + d, zl) < 3)(columns_copy(d).start)
    load[1].wait()
    for h in (0, 1):
        ring_send(1, h, 1)

    me = y * 2 + c
    sbuf[me] = jnp.full((8, 128), strength[0], F32)
    others = [(d, b) for d in range(4) for b in range(2) if d or b]

    def strengths_copy(d, b):
        n = d * 2 + b
        return remote(sbuf.at[me], sbuf.at[me], s_snd.at[n], s_rcv.at[n], yc_id(d, b))

    for d, b in others:
        strengths_copy(d, b).start()

    rows = pl.ds(pl.multiple_of(c * 64, 64), 64)
    cols = pl.ds(pl.multiple_of(y * 1024, 1024), 1024)
    mine = pl.ds(pl.multiple_of(x * 64, 64), 64)
    pgb[mine, :] = (prompt[rows, :].astype(F32) * gain[...]).astype(BF16)

    def prompt_copy(d):
        return remote(pgb.at[mine, :], pgb.at[mine, :], p_snd.at[d], p_rcv.at[d], x_id(d))

    for d in (1, 2, 3):
        prompt_copy(d).start()
    steered = steer[...] * gain[...]
    high = steered.astype(BF16).astype(F32)
    which = lax.broadcasted_iota(jnp.int32, (16, D), 0)
    pgb[256:272, :] = jnp.where(which == 0, high, jnp.where(which == 1, steered - high, 0.0)).astype(BF16)

    qb[y] = jnp.zeros((4, 8, 256), F32)
    held(0, 0, columns_own().wait)
    for d in (1, 2, 3):
        held(0, 0, columns_copy(d).wait_recv)
    for h in (0, 1):
        ring_send(0, h, 1)
    for h in (0, 1):
        sibling_send(0, h, 0)
    load[2].wait()
    for p in (1, 2):
        for h in (0, 1):
            sibling_send(p, h, 0)

    for d, b in others:
        strengths_copy(d, b).wait()
    lane = lax.broadcasted_iota(jnp.int32, (64, 128), 1)
    table = jnp.zeros((64, 128), F32)
    by_row[0] = jnp.transpose(ids[...].astype(F32))
    by_row[1] = jnp.transpose(gates[...])
    name = by_row[0, rows, :].astype(jnp.int32)
    weight = by_row[1, rows, :]
    for k in range(8):
        table = table + jnp.where(lane == name[:, k:k + 1], weight[:, k:k + 1], 0.0)
    misc[x] = table

    @pl.loop(0, 8)
    def _(j):
        s = sbuf[j][0:1, 0:1]
        square = jnp.zeros((64, 128), F32)
        for n in range(32):
            here = slice(n * 128, (n + 1) * 128)
            piece = prompt[rows, here].astype(F32) + s * steer[:, here]
            square = square + piece * piece
        mean = jnp.sum(square, axis=1, keepdims=True) * (1.0 / D)
        misc[x] = misc[x] + jnp.where(lane == 16 + j, lax.rsqrt(mean + epsilon), 0.0)

    def misc_copy(d):
        return remote(misc.at[x], misc.at[x], m_snd.at[d], m_rcv.at[d], x_id(d))

    for d in (1, 2, 3):
        misc_copy(d).start()
    ring_take(0, 1)

    def turn(i):
        return lax.rem(zl + TURN[i], 4)

    def expert(i):
        e = turn(i)
        b = column(y, e)

        @pl.when(b < 3)
        def _():
            for n in ((3, 4), (2, 5), (1, 6), (0, 7))[i]:
                for h in (0, 1):
                    sibling(0, h, n).wait_recv()
            upper = jnp.dot(pgb[...], ub[e].reshape(D, 256), preferred_element_type=F32)
            here = pl.ds(pl.multiple_of(b * 256, 256), 256)
            for block in range(4):
                ab[block, e, :, here] = upper[block * 64:(block + 1) * 64].astype(BF16)
            qb[y, e] = upper[256:257] + upper[257:258] + jnp.zeros((8, 256), F32)
            for d in (1, 3):
                gather_copy(i, d).start()

    def owner(d):
        return y + (0 if d in (1, 3) else 3 if d == 2 else 1)

    def gather_copy(i, d):
        e = turn(i)
        here = pl.ds(pl.multiple_of(lax.rem(column(owner(d), e), 3) * 256, 256), 256)
        blocks = pl.ds(0, 4) if d in (1, 3) else pl.ds(0, 2) if d == 2 else pl.ds(2, 2)
        piece = ab.at[blocks, e, :, here]
        return remote(piece, piece, ag_snd.at[i, d], ag_rcv.at[i, d], yc_id((3, 1, 1, 3)[d], 0))

    def sent(i, d, fn):
        pl.when(column(owner(d), turn(i)) < 3)(fn)

    def came(i, d, fn):
        pl.when(column(y + (2, 3, 2, 1)[d], turn(i)) < 3)(fn)

    def forward(i):
        came(i, 1, gather_copy(i, 1).wait_recv)
        sent(i, 2, gather_copy(i, 2).start)
        came(i, 3, gather_copy(i, 3).wait_recv)
        sent(i, 0, gather_copy(i, 0).start)

    def push_copy(d):
        return remote(qb.at[y], qb.at[y], q_snd.at[d], q_rcv.at[d], yc_id(d, 0))

    for d in (1, 2, 3):
        misc_copy(d).wait_recv()

    @pl.loop(0, 4)
    def _(block):
        here = misc[block]
        for e in range(4):
            column = jnp.sum(jnp.where(lane == e * 4 + x, here, 0.0), axis=1, keepdims=True)
            gt[block, e] = jnp.broadcast_to(column, (64, 128))
        for j in range(8):
            it[block, j] = jnp.broadcast_to(0.5 * here[:, 16 + j:17 + j], (64, 128))

    ring_take(0, 2)
    for d in (1, 2, 3):
        prompt_copy(d).wait_recv()
    expert(0)
    ring_take(0, 3)
    ring_take(1, 1)
    expert(1)
    expert(2)
    forward(0)
    ring_take(0, 4)
    expert(3)
    for d in (1, 2, 3):
        push_copy(d).start()
    ring_take(1, 2)
    forward(1)
    forward(2)
    ring_take(1, 3)
    for h in (0, 1):
        ring_send(2, h, 1)
    forward(3)
    ring_take(1, 4)
    for i in range(4):
        for d in (0, 2):
            came(i, d, gather_copy(i, d).wait_recv)
    for d in (1, 2, 3):
        push_copy(d).wait_recv()

    @pl.loop(0, 4)
    def _(e):
        for b in range(3):
            push = qb[lax.rem(e + b, 4), e]
            for j in range(8):
                sq[j, e, :, b * 256:(b + 1) * 256] = push * sbuf[j][:, 0:1]

    def hidden(g):
        dest_y = lax.rem(y + g + 1, 4)

        @pl.loop(0, 16)
        def _(n):
            block, e = n // 4, lax.rem(n, 4)
            gate = gt[block, e]
            for b in range(2):
                j = dest_y * 2 + b
                inv = it[block, j]
                for m in range(6):
                    here = slice(m * 128, (m + 1) * 128)
                    pre = ab[block, e, :, here].astype(F32).reshape(8, 8, 128) + sq[j, e, :, here][None]
                    half = pre.reshape(64, 128) * inv
                    value = (half * gate) * (1.0 + jnp.tanh(half))
                    hb[g, pl.ds(pl.multiple_of(block * 128 + b * 64, 64), 64),
                       pl.ds(pl.multiple_of(e * EH + m * 128, 128), 128)] = value.astype(BF16)

    def passed(p):
        for h in (0, 1):
            for n in range(8):
                sibling(p, h, n).wait_recv()

    def relay(u, way):
        return remote(
            rsend.at[u, way], rrecv.at[u, way], rl_snd.at[u, way], rl_rcv.at[u, way], x_id(1 + 2 * way)
        )

    def main(u, way):
        return remote(
            msend.at[u, way], mrecv.at[u, way], mn_snd.at[u, way], mn_rcv.at[u, way], x_id(1 + 2 * way)
        )

    def final(g, b):
        return remote(
            fin.at[g, pl.ds(pl.multiple_of(lax.rem(c + b, 2) * 64, 64), 64), :],
            out.at[0, rows, cols], f_snd.at[g, b], f_rcv.at[g, b], yc_id(g + 1, b),
        )

    def final_local():
        return pltpu.make_async_copy(fin.at[3, rows, :], out.at[0, rows, cols], f_loc)

    def multiply(u, half):
        g = lax.rem(u, 4)

        @pl.loop(0, 2)
        def _(way):
            sums = jnp.dot(hb[g], db[half, way], preferred_element_type=F32)
            place = pl.ds(pl.multiple_of(way * 256, 256), 256)
            for block in range(4):
                part[u, block, :, place] = sums[block * 128:(block + 1) * 128]
            rsend[u, way] = part[u, lax.rem(x + 2, 4), :, place].astype(BF16)
            relay(u, way).start()

    def pass_on(u):
        for way in (0, 1):
            relay(u, way).wait_recv()
            block = lax.rem(x + 1 + 2 * way, 4)
            same = slice(way * 256, way * 256 + 256)
            other = slice(256 - way * 256, 512 - way * 256)
            msend[u, way, :, same] = (part[u, block, :, same] + rrecv[u, way].astype(F32)).astype(BF16)
            msend[u, way, :, other] = part[u, block, :, other].astype(BF16)
            main(u, way).start()

    def finish(u, half):
        g = lax.rem(u, 4)
        main(u, 0).wait_recv()
        main(u, 1).wait_recv()
        for n in range(4):
            here = slice(n * 128, n * 128 + 128)
            fin[g, :, n * 256 + half * 128:n * 256 + half * 128 + 128] = (
                part[u, x, :, here] + mrecv[u, 0, :, here].astype(F32) + mrecv[u, 1, :, here].astype(F32)
            ).astype(BF16)

    ring_take(2, 1)
    hidden(0)
    passed(1)
    multiply(0, 0)
    ring_take(2, 2)
    hidden(1)
    multiply(1, 0)
    ring_take(2, 3)
    pass_on(0)
    hidden(2)
    ring_take(2, 4)
    multiply(2, 0)
    pass_on(1)
    finish(0, 0)
    hidden(3)
    multiply(3, 0)
    pass_on(2)
    finish(1, 0)
    passed(2)

    @pl.loop(4, 10)
    def _(t):
        @pl.when(t < 8)
        def _():
            multiply(t, 1)

        @pl.when(t < 9)
        def _():
            pass_on(t - 1)

        @pl.when(t < 6)
        def _():
            finish(t - 2, 0)

        @pl.when(t >= 6)
        def _():
            finish(t - 2, 1)
            g = t - 6
            final(g, 1).start()

            @pl.when(g < 3)
            def _():
                final(g, 0).start()

            @pl.when(g == 3)
            def _():
                final_local().start()

    for d in (1, 2, 3):
        prompt_copy(d).wait_send()
        misc_copy(d).wait_send()
        push_copy(d).wait_send()
        pl.when(column(y + d, zl) < 3)(columns_copy(d).wait_send)
    for i in range(4):
        for d in range(4):
            sent(i, d, gather_copy(i, d).wait_send)
    for p in range(3):
        for h in (0, 1):
            for k in (1, 2, 3, 4):
                for way in ways(h, k):
                    held(p, (k - 1) * (2 * way - 1), ring(p, h, way, k).wait_send)
            for n in range(8):
                held(p, sibling_step(n), sibling(p, h, n).wait_send)
    for u in range(8):
        for way in (0, 1):
            relay(u, way).wait_send()
            main(u, way).wait_send()
    for g in range(4):
        for b in (0, 1):
            if (g, b) != (3, 0):
                final(g, b).wait()
    final_local().wait()


def local(prompt, steer_vec, strengths, norm_gain, expert_ids, gate_values, up_weight, down_weight):
    vmem = pl.BlockSpec(memory_space=pltpu.VMEM)
    away = pl.BlockSpec(memory_space=pl.ANY)
    dma = pltpu.SemaphoreType.DMA
    return pl.pallas_call(
        kernel,
        out_shape=jax.ShapeDtypeStruct((1, 128, D), BF16),
        in_specs=[vmem, vmem, pl.BlockSpec(memory_space=pltpu.SMEM)] + [vmem] * 4 + [away],
        out_specs=away,
        scratch_shapes=[
            pltpu.VMEM((8, 8, 128), F32),
            pltpu.VMEM((2, 128, 8), F32),
            pltpu.VMEM((272, D), BF16),
            pltpu.VMEM((4, 64, 128), F32),
            pltpu.VMEM((4, 4, 64, 128), F32),
            pltpu.VMEM((4, 8, 64, 128), F32),
            pltpu.VMEM((8, 4, 8, EH), F32),
            pltpu.VMEM((4, 4, 2, 2, 256, 256), BF16),
            pltpu.VMEM((2, 2, 4 * EH, 256), BF16),
            pltpu.VMEM((4, 4, 64, EH), BF16),
            pltpu.VMEM((4, 4, 8, 256), F32),
            pltpu.VMEM((4, 512, 4 * EH), BF16),
            pltpu.VMEM((8, 4, 128, 512), F32),
            pltpu.VMEM((8, 2, 128, 256), BF16),
            pltpu.VMEM((8, 2, 128, 256), BF16),
            pltpu.VMEM((8, 2, 128, 512), BF16),
            pltpu.VMEM((8, 2, 128, 512), BF16),
            pltpu.VMEM((4, 128, 1024), BF16),
            dma((3,)),
            dma((8,)), dma((8,)),
            dma((4,)), dma((4,)),
            dma((4,)), dma((4,)),
            dma((3, 2, 2, 4)), dma((3, 2, 2, 4)),
            dma((3, 2, 8)), dma((3, 2, 8)),
            dma((4,)), dma((4,)), dma(()),
            dma((4, 4)), dma((4, 4)),
            dma((4,)), dma((4,)),
            dma((8, 2)), dma((8, 2)),
            dma((8, 2)), dma((8, 2)),
            dma((4, 2)), dma((4, 2)),
            dma(()),
        ],
        compiler_params=pltpu.CompilerParams(
            collective_id=0, has_side_effects=True, vmem_limit_bytes=60 * 1024 * 1024
        ),
        cost_estimate=pl.CostEstimate(flops=18_000_000_000, bytes_accessed=3_000_000, transcendentals=6_300_000),
    )(
        prompt,
        steer_vec[None],
        strengths,
        norm_gain[None],
        expert_ids.T,
        gate_values.T,
        up_weight[0],
        down_weight[0],
    )


def solution(mesh):
    fine = Mesh(mesh.devices.reshape(4, 2, 2, 4, 4), ("y", "zh", "c", "zl", "x"))
    return jax.shard_map(
        local,
        mesh=fine,
        in_specs=(
            P(EXPERT, None),
            P(),
            P(WIDE),
            P(),
            P(EXPERT, None),
            P(EXPERT, None),
            P(EXPERT, WIDE, None),
            P(EXPERT, None, WIDE),
        ),
        out_specs=P(WIDE, EXPERT, None),
        check_vma=False,
    )
```

```python
import jax
import jax.numpy as jnp
from jax import lax
from jax.experimental import pallas as pl
from jax.experimental.pallas import tpu as pltpu
from jax.sharding import Mesh, PartitionSpec as P

D = 4096
EH = 768
epsilon = 1e-06

WIDE = ("y", "zh", "c")
EXPERT = ("zl", "x")
MESH = pl.DeviceIdType.MESH
F32 = jnp.float32
BF16 = jnp.bfloat16
TURN = (2, 1, 3, 0)


def kernel(
    prompt, steer, strength, gain, ids, gates, up, down, out,
    sbuf, by_row, pgb, misc, gt, it, sq, ub, db, ab, qb, hb, part, rsend, rrecv, msend, mrecv, fin,
    load_sem, s_snd, s_rcv, p_snd, p_rcv, m_snd, m_rcv, ring_snd, ring_rcv, sib_snd, sib_rcv,
    a_snd, a_rcv, a_loc, ag_snd, ag_rcv, q_snd, q_rcv, rl_snd, rl_rcv, mn_snd, mn_rcv, f_snd, f_rcv, f_loc,
):
    y, zh, c = lax.axis_index("y"), lax.axis_index("zh"), lax.axis_index("c")
    zl, x = lax.axis_index("zl"), lax.axis_index("x")
    zz = zh * 4 + zl
    sib = 1 - c

    def at_z(step):
        z = lax.rem(zz + step + 8, 8)
        return z // 4, lax.rem(z, 4)

    def z_id(step):
        a, b = at_z(step)
        return {"zh": a, "zl": b}

    def x_id(d):
        return {"x": lax.rem(x + d, 4)}

    def yc_id(d, b):
        return {"y": lax.rem(y + d, 4), "c": lax.rem(c + b, 2)}

    def remote(src, dst, snd, rcv, dev):
        return pltpu.make_async_remote_copy(
            src_ref=src, dst_ref=dst, send_sem=snd, recv_sem=rcv, device_id=dev, device_id_type=MESH
        )

    def column(at_y, e):
        return lax.rem(at_y - e + 8, 4)

    def slot(p, step, core, h):
        a, b = at_z(step)
        if p == 0:
            return ub.at[b, pl.ds(2 * h, 2), a, core]
        return db.at[p - 1, a, pl.ds(pl.multiple_of(b * EH + h * 384, 128), 384),
                     pl.ds(pl.multiple_of(core * 128, 128), 128)]

    def held(p, step, fn):
        if p:
            fn()
        else:
            pl.when(column(y, at_z(step)[1]) < 3)(fn)

    load = [None]
    for p in (0, 1):
        load.append(pltpu.make_async_copy(
            down.at[:, p * 128:(p + 1) * 128],
            db.at[p, zh, pl.ds(pl.multiple_of(zl * EH, 128), EH), pl.ds(pl.multiple_of(c * 128, 128), 128)],
            load_sem.at[1 + p],
        ))
    for cp in load[1:]:
        cp.start()

    partners = [z_id(1), z_id(-1)] + [x_id(d) for d in (1, 2, 3)]
    partners += [yc_id(d, b) for d in range(4) for b in range(2) if d or b]
    barrier = pltpu.get_barrier_semaphore()
    for dev in partners:
        pl.semaphore_signal(barrier, inc=1, device_id=dev, device_id_type=MESH)
    pl.semaphore_wait(barrier, len(partners))

    def ring(p, h, way, k):
        sign = 1 if way == 0 else -1
        piece = slot(p, -sign * (k - 1), c, h)
        return remote(piece, piece, ring_snd.at[p, h, way, k - 1], ring_rcv.at[p, h, way, k - 1], z_id(sign))

    def ways(h, k):
        return (0, 1) if k < 4 else (h,)

    def ring_send(p, h, k):
        for way in ways(h, k):
            held(p, (k - 1) * (2 * way - 1), ring(p, h, way, k).start)

    def sibling_step(n):
        return (0, -1, 1, -2, 2, -3, 3, 4)[n]

    def sibling(p, h, n):
        piece = slot(p, sibling_step(n), c, h)
        return remote(piece, piece, sib_snd.at[p, h, n], sib_rcv.at[p, h, n], {"c": sib})

    def sibling_send(p, h, n):
        held(p, sibling_step(n), sibling(p, h, n).start)

    def ring_take(p, k):
        for h in (0, 1):
            for way in ways(h, k):
                held(p, k * (2 * way - 1), ring(p, h, way, k).wait_recv)
            if k < 4:
                ring_send(p, h, k + 1)
                sibling_send(p, h, 2 * k - 1)
                sibling_send(p, h, 2 * k)
            else:
                sibling_send(p, h, 7)

    def columns_copy(d):
        b = lax.rem(column(y + d, zl), 3)
        return remote(
            up.at[:, pl.ds(pl.multiple_of(b * 256, 256), 256)], ub.at[zl, y, zh, c],
            a_snd.at[d], a_rcv.at[d], yc_id(d, 0),
        )

    def columns_own():
        b = lax.rem(column(y, zl), 3)
        return pltpu.make_async_copy(
            up.at[:, pl.ds(pl.multiple_of(b * 256, 256), 256)], ub.at[zl, y, zh, c], a_loc
        )

    held(0, 0, columns_own().start)
    for d in (1, 2, 3):
        pl.when(column(y + d, zl) < 3)(columns_copy(d).start)
    load[1].wait()
    for h in (0, 1):
        ring_send(1, h, 1)

    me = y * 2 + c
    sbuf[me] = jnp.full((8, 128), strength[0], F32)
    others = [(d, b) for d in range(4) for b in range(2) if d or b]

    def strengths_copy(d, b):
        n = d * 2 + b
        return remote(sbuf.at[me], sbuf.at[me], s_snd.at[n], s_rcv.at[n], yc_id(d, b))

    for d, b in others:
        strengths_copy(d, b).start()

    rows = pl.ds(pl.multiple_of(c * 64, 64), 64)
    cols = pl.ds(pl.multiple_of(y * 1024, 1024), 1024)
    mine = pl.ds(pl.multiple_of(x * 64, 64), 64)
    pgb[mine, :] = (prompt[rows, :].astype(F32) * gain[...]).astype(BF16)

    def prompt_copy(d):
        return remote(pgb.at[mine, :], pgb.at[mine, :], p_snd.at[d], p_rcv.at[d], x_id(d))

    for d in (1, 2, 3):
        prompt_copy(d).start()
    steered = steer[...] * gain[...]
    high = steered.astype(BF16).astype(F32)
    which = lax.broadcasted_iota(jnp.int32, (16, D), 0)
    pgb[256:272, :] = jnp.where(which == 0, high, jnp.where(which == 1, steered - high, 0.0)).astype(BF16)

    load[2].wait()
    for p in (1, 2):
        for h in (0, 1):
            sibling_send(p, h, 0)
    held(0, 0, columns_own().wait)
    for d in (1, 2, 3):
        held(0, 0, columns_copy(d).wait_recv)
    ring_send(0, 0, 1)
    for h in (0, 1):
        sibling_send(0, h, 0)

    for d, b in others:
        strengths_copy(d, b).wait()
    lane = lax.broadcasted_iota(jnp.int32, (64, 128), 1)
    table = jnp.zeros((64, 128), F32)
    by_row[0] = jnp.transpose(ids[...].astype(F32))
    by_row[1] = jnp.transpose(gates[...])
    name = by_row[0, rows, :].astype(jnp.int32)
    weight = by_row[1, rows, :]
    for k in range(8):
        table = table + jnp.where(lane == name[:, k:k + 1], weight[:, k:k + 1], 0.0)
    misc[x] = table

    @pl.loop(0, 8)
    def _(j):
        s = sbuf[j][0:1, 0:1]
        square = jnp.zeros((64, 128), F32)
        for n in range(32):
            here = slice(n * 128, (n + 1) * 128)
            piece = prompt[rows, here].astype(F32) + s * steer[:, here]
            square = square + piece * piece
        mean = jnp.sum(square, axis=1, keepdims=True) * (1.0 / D)
        misc[x] = misc[x] + jnp.where(lane == 16 + j, lax.rsqrt(mean + epsilon), 0.0)

    def misc_copy(d):
        return remote(misc.at[x], misc.at[x], m_snd.at[d], m_rcv.at[d], x_id(d))

    for d in (1, 2, 3):
        misc_copy(d).start()
    for way in (0, 1):
        held(0, 0, ring(0, 0, way, 1).wait_send)
    ring_send(0, 1, 1)
    ring_take(0, 1)

    def turn(i):
        return lax.rem(zl + TURN[i], 4)

    def expert(i):
        e = turn(i)
        b = column(y, e)

        @pl.when(b < 3)
        def _():
            for n in ((3, 4), (2, 5), (1, 6), (0, 7))[i]:
                for h in (0, 1):
                    sibling(0, h, n).wait_recv()
            upper = jnp.dot(pgb[...], ub[e].reshape(D, 256), preferred_element_type=F32)
            here = pl.ds(pl.multiple_of(b * 256, 256), 256)
            for block in range(4):
                ab[block, e, :, here] = upper[block * 64:(block + 1) * 64].astype(BF16)
            qb[y, e] = upper[256:257] + upper[257:258] + jnp.zeros((8, 256), F32)
            for d in (1, 3):
                gather_copy(i, d).start()
            for d in (1, 2, 3):
                push_copy(i, d).start()

    def owner(d):
        return y + (0 if d in (1, 3) else 3 if d == 2 else 1)

    def gather_copy(i, d):
        e = turn(i)
        here = pl.ds(pl.multiple_of(lax.rem(column(owner(d), e), 3) * 256, 256), 256)
        blocks = pl.ds(0, 4) if d in (1, 3) else pl.ds(0, 2) if d == 2 else pl.ds(2, 2)
        piece = ab.at[blocks, e, :, here]
        return remote(piece, piece, ag_snd.at[i, d], ag_rcv.at[i, d], yc_id((3, 1, 1, 3)[d], 0))

    def sent(i, d, fn):
        pl.when(column(owner(d), turn(i)) < 3)(fn)

    def came(i, d, fn):
        pl.when(column(y + (2, 3, 2, 1)[d], turn(i)) < 3)(fn)

    def forward(i):
        came(i, 1, gather_copy(i, 1).wait_recv)
        sent(i, 2, gather_copy(i, 2).start)
        came(i, 3, gather_copy(i, 3).wait_recv)
        sent(i, 0, gather_copy(i, 0).start)

    def push_copy(i, d):
        piece = qb.at[y, turn(i)]
        return remote(piece, piece, q_snd.at[i, d], q_rcv.at[i, d], yc_id(d, 0))

    for d in (1, 2, 3):
        misc_copy(d).wait_recv()

    @pl.loop(0, 4)
    def _(block):
        here = misc[block]
        for e in range(4):
            column = jnp.sum(jnp.where(lane == e * 4 + x, here, 0.0), axis=1, keepdims=True)
            gt[block, e] = jnp.broadcast_to(column, (64, 128))
        for j in range(8):
            it[block, j] = jnp.broadcast_to(0.5 * here[:, 16 + j:17 + j], (64, 128))

    def gathered(i):
        e = turn(i)
        for d in (0, 2):
            came(i, d, gather_copy(i, d).wait_recv)
        for d in (1, 2, 3):
            pl.when(column(y + 4 - d, e) < 3)(push_copy(i, d).wait_recv)
        for b in range(3):
            push = qb[lax.rem(e + b, 4), e]
            for j in range(8):
                sq[j, e, :, b * 256:(b + 1) * 256] = push * sbuf[j][:, 0:1]

        @pl.loop(0, 16)
        def _(n):
            block, g = n // 4, lax.rem(n, 4)
            gate = gt[block, e]
            for b in range(2):
                j = lax.rem(y + g + 1, 4) * 2 + b
                inv = it[block, j]
                for m in range(6):
                    here = slice(m * 128, (m + 1) * 128)
                    pre = ab[block, e, :, here].astype(F32).reshape(8, 8, 128) + sq[j, e, :, here][None]
                    half = pre.reshape(64, 128) * inv
                    value = (half * gate) * (1.0 + jnp.tanh(half))
                    hb[g, pl.ds(pl.multiple_of(block * 128 + b * 64, 64), 64),
                       pl.ds(pl.multiple_of(e * EH + m * 128, 128), 128)] = value.astype(BF16)

    ring_take(0, 2)
    ring_take(1, 1)
    for d in (1, 2, 3):
        prompt_copy(d).wait_recv()
    expert(0)
    ring_take(0, 3)
    ring_take(1, 2)
    expert(1)
    expert(2)
    forward(0)
    ring_take(0, 4)
    expert(3)
    ring_take(1, 3)
    for h in (0, 1):
        ring_send(2, h, 1)
    forward(1)
    forward(2)
    gathered(0)
    forward(3)
    ring_take(1, 4)
    gathered(1)
    ring_take(2, 1)
    gathered(2)
    gathered(3)
    ring_take(2, 2)

    def passed(p):
        for h in (0, 1):
            for n in range(8):
                sibling(p, h, n).wait_recv()

    def relay(u, way):
        return remote(
            rsend.at[u, way], rrecv.at[u, way], rl_snd.at[u, way], rl_rcv.at[u, way], x_id(1 + 2 * way)
        )

    def main(u, way):
        return remote(
            msend.at[u, way], mrecv.at[u, way], mn_snd.at[u, way], mn_rcv.at[u, way], x_id(1 + 2 * way)
        )

    def final(g, b):
        return remote(
            fin.at[g, pl.ds(pl.multiple_of(lax.rem(c + b, 2) * 64, 64), 64), :],
            out.at[0, rows, cols], f_snd.at[g, b], f_rcv.at[g, b], yc_id(g + 1, b),
        )

    def final_local():
        return pltpu.make_async_copy(fin.at[3, rows, :], out.at[0, rows, cols], f_loc)

    def multiply(u, half):
        g = lax.rem(u, 4)

        @pl.loop(0, 2)
        def _(way):
            sums = jnp.dot(hb[g], db[half, way], preferred_element_type=F32)
            place = pl.ds(pl.multiple_of(way * 256, 256), 256)
            for block in range(4):
                part[u, block, :, place] = sums[block * 128:(block + 1) * 128]
            rsend[u, way] = part[u, lax.rem(x + 2, 4), :, place].astype(BF16)
            relay(u, way).start()

    def pass_on(u):
        for way in (0, 1):
            relay(u, way).wait_recv()
            block = lax.rem(x + 1 + 2 * way, 4)
            same = slice(way * 256, way * 256 + 256)
            other = slice(256 - way * 256, 512 - way * 256)
            msend[u, way, :, same] = (part[u, block, :, same] + rrecv[u, way].astype(F32)).astype(BF16)
            msend[u, way, :, other] = part[u, block, :, other].astype(BF16)
            main(u, way).start()

    def finish(u, half):
        g = lax.rem(u, 4)
        main(u, 0).wait_recv()
        main(u, 1).wait_recv()
        for n in range(4):
            here = slice(n * 128, n * 128 + 128)
            fin[g, :, n * 256 + half * 128:n * 256 + half * 128 + 128] = (
                part[u, x, :, here] + mrecv[u, 0, :, here].astype(F32) + mrecv[u, 1, :, here].astype(F32)
            ).astype(BF16)

    passed(1)
    multiply(0, 0)
    ring_take(2, 3)
    multiply(1, 0)
    pass_on(0)
    ring_take(2, 4)

    @pl.loop(2, 4)
    def _(t):
        multiply(t, 0)
        pass_on(t - 1)
        finish(t - 2, 0)

    passed(2)

    @pl.loop(4, 10)
    def _(t):
        @pl.when(t < 8)
        def _():
            multiply(t, 1)

        @pl.when(t < 9)
        def _():
            pass_on(t - 1)

        @pl.when(t < 6)
        def _():
            finish(t - 2, 0)

        @pl.when(t >= 6)
        def _():
            finish(t - 2, 1)
            g = t - 6
            final(g, 1).start()

            @pl.when(g < 3)
            def _():
                final(g, 0).start()

            @pl.when(g == 3)
            def _():
                final_local().start()

    for d in (1, 2, 3):
        prompt_copy(d).wait_send()
        misc_copy(d).wait_send()
        pl.when(column(y + d, zl) < 3)(columns_copy(d).wait_send)
    for i in range(4):
        for d in (1, 2, 3):
            sent(i, 1, push_copy(i, d).wait_send)
        for d in range(4):
            sent(i, d, gather_copy(i, d).wait_send)
    for p in range(3):
        for h in (0, 1):
            for k in (1, 2, 3, 4):
                for way in ways(h, k):
                    if (p, h, k) != (0, 0, 1):
                        held(p, (k - 1) * (2 * way - 1), ring(p, h, way, k).wait_send)
            for n in range(8):
                held(p, sibling_step(n), sibling(p, h, n).wait_send)
    for u in range(8):
        for way in (0, 1):
            relay(u, way).wait_send()
            main(u, way).wait_send()
    for g in range(4):
        for b in (0, 1):
            if (g, b) != (3, 0):
                final(g, b).wait()
    final_local().wait()


def local(prompt, steer_vec, strengths, norm_gain, expert_ids, gate_values, up_weight, down_weight):
    vmem = pl.BlockSpec(memory_space=pltpu.VMEM)
    away = pl.BlockSpec(memory_space=pl.ANY)
    dma = pltpu.SemaphoreType.DMA
    return pl.pallas_call(
        kernel,
        out_shape=jax.ShapeDtypeStruct((1, 128, D), BF16),
        in_specs=[vmem, vmem, pl.BlockSpec(memory_space=pltpu.SMEM)] + [vmem] * 4 + [away],
        out_specs=away,
        scratch_shapes=[
            pltpu.VMEM((8, 8, 128), F32),
            pltpu.VMEM((2, 128, 8), F32),
            pltpu.VMEM((272, D), BF16),
            pltpu.VMEM((4, 64, 128), F32),
            pltpu.VMEM((4, 4, 64, 128), F32),
            pltpu.VMEM((4, 8, 64, 128), F32),
            pltpu.VMEM((8, 4, 8, EH), F32),
            pltpu.VMEM((4, 4, 2, 2, 256, 256), BF16),
            pltpu.VMEM((2, 2, 4 * EH, 256), BF16),
            pltpu.VMEM((4, 4, 64, EH), BF16),
            pltpu.VMEM((4, 4, 8, 256), F32),
            pltpu.VMEM((4, 512, 4 * EH), BF16),
            pltpu.VMEM((8, 4, 128, 512), F32),
            pltpu.VMEM((8, 2, 128, 256), BF16),
            pltpu.VMEM((8, 2, 128, 256), BF16),
            pltpu.VMEM((8, 2, 128, 512), BF16),
            pltpu.VMEM((8, 2, 128, 512), BF16),
            pltpu.VMEM((4, 128, 1024), BF16),
            dma((3,)),
            dma((8,)), dma((8,)),
            dma((4,)), dma((4,)),
            dma((4,)), dma((4,)),
            dma((3, 2, 2, 4)), dma((3, 2, 2, 4)),
            dma((3, 2, 8)), dma((3, 2, 8)),
            dma((4,)), dma((4,)), dma(()),
            dma((4, 4)), dma((4, 4)),
            dma((4, 4)), dma((4, 4)),
            dma((8, 2)), dma((8, 2)),
            dma((8, 2)), dma((8, 2)),
            dma((4, 2)), dma((4, 2)),
            dma(()),
        ],
        compiler_params=pltpu.CompilerParams(
            collective_id=0, has_side_effects=True, vmem_limit_bytes=60 * 1024 * 1024
        ),
        cost_estimate=pl.CostEstimate(flops=18_000_000_000, bytes_accessed=3_000_000, transcendentals=6_300_000),
    )(
        prompt,
        steer_vec[None],
        strengths,
        norm_gain[None],
        expert_ids.T,
        gate_values.T,
        up_weight[0],
        down_weight[0],
    )


def solution(mesh):
    fine = Mesh(mesh.devices.reshape(4, 2, 2, 4, 4), ("y", "zh", "c", "zl", "x"))
    return jax.shard_map(
        local,
        mesh=fine,
        in_specs=(
            P(EXPERT, None),
            P(),
            P(WIDE),
            P(),
            P(EXPERT, None),
            P(EXPERT, None),
            P(EXPERT, WIDE, None),
            P(EXPERT, None, WIDE),
        ),
        out_specs=P(WIDE, EXPERT, None),
        check_vma=False,
    )
```

```python
import jax
import jax.numpy as jnp
from jax import lax
from jax.experimental import pallas as pl
from jax.experimental.pallas import tpu as pltpu
from jax.sharding import Mesh, PartitionSpec as P

D = 4096
EH = 768
epsilon = 1e-06

WIDE = ("y", "zh", "c")
EXPERT = ("zl", "x")
MESH = pl.DeviceIdType.MESH
F32 = jnp.float32
BF16 = jnp.bfloat16
TURN = (2, 1, 3, 0)


def kernel(
    prompt, steer, strength, gain, ids, gates, up, down, out,
    sbuf, by_row, pgb, misc, gt, it, sq, ub, db, ab, qb, hb, part, rsend, rrecv, msend, mrecv, fin,
    load_sem, s_snd, s_rcv, p_snd, p_rcv, m_snd, m_rcv, ring_snd, ring_rcv, sib_snd, sib_rcv,
    a_snd, a_rcv, a_loc, ag_snd, ag_rcv, q_snd, q_rcv, rl_snd, rl_rcv, mn_snd, mn_rcv, f_snd, f_rcv, f_loc,
):
    y, zh, c = lax.axis_index("y"), lax.axis_index("zh"), lax.axis_index("c")
    zl, x = lax.axis_index("zl"), lax.axis_index("x")
    zz = zh * 4 + zl
    sib = 1 - c

    def at_z(step):
        z = lax.rem(zz + step + 8, 8)
        return z // 4, lax.rem(z, 4)

    def z_id(step):
        a, b = at_z(step)
        return {"zh": a, "zl": b}

    def x_id(d):
        return {"x": lax.rem(x + d, 4)}

    def yc_id(d, b):
        return {"y": lax.rem(y + d, 4), "c": lax.rem(c + b, 2)}

    def remote(src, dst, snd, rcv, dev):
        return pltpu.make_async_remote_copy(
            src_ref=src, dst_ref=dst, send_sem=snd, recv_sem=rcv, device_id=dev, device_id_type=MESH
        )

    def column(at_y, e):
        return lax.rem(at_y - e + 8, 4)

    def slot(p, step, core, h):
        a, b = at_z(step)
        if p == 0:
            return ub.at[b, pl.ds(2 * h, 2), a, core]
        return db.at[p - 1, a, pl.ds(pl.multiple_of(b * EH + h * 384, 128), 384),
                     pl.ds(pl.multiple_of(core * 128, 128), 128)]

    def held(p, step, fn):
        if p:
            fn()
        else:
            pl.when(column(y, at_z(step)[1]) < 3)(fn)

    load = [None]
    for p in (0, 1):
        load.append(pltpu.make_async_copy(
            down.at[:, p * 128:(p + 1) * 128],
            db.at[p, zh, pl.ds(pl.multiple_of(zl * EH, 128), EH), pl.ds(pl.multiple_of(c * 128, 128), 128)],
            load_sem.at[1 + p],
        ))
    for cp in load[1:]:
        cp.start()

    partners = [z_id(1), z_id(-1)] + [x_id(d) for d in (1, 2, 3)]
    partners += [yc_id(d, b) for d in range(4) for b in range(2) if d or b]
    barrier = pltpu.get_barrier_semaphore()
    for dev in partners:
        pl.semaphore_signal(barrier, inc=1, device_id=dev, device_id_type=MESH)
    pl.semaphore_wait(barrier, len(partners))

    def ring(p, h, way, k):
        sign = 1 if way == 0 else -1
        piece = slot(p, -sign * (k - 1), c, h)
        return remote(piece, piece, ring_snd.at[p, h, way, k - 1], ring_rcv.at[p, h, way, k - 1], z_id(sign))

    def ways(h, k):
        return (0, 1) if k < 4 else (h,)

    def ring_send(p, h, k):
        for way in ways(h, k):
            held(p, (k - 1) * (2 * way - 1), ring(p, h, way, k).start)

    def sibling_step(n):
        return (0, -1, 1, -2, 2, -3, 3, 4)[n]

    def sibling(p, h, n):
        piece = slot(p, sibling_step(n), c, h)
        return remote(piece, piece, sib_snd.at[p, h, n], sib_rcv.at[p, h, n], {"c": sib})

    def sibling_send(p, h, n):
        held(p, sibling_step(n), sibling(p, h, n).start)

    def ring_take(p, k):
        for h in (0, 1):
            for way in ways(h, k):
                held(p, k * (2 * way - 1), ring(p, h, way, k).wait_recv)
            if k < 4:
                ring_send(p, h, k + 1)
                sibling_send(p, h, 2 * k - 1)
                sibling_send(p, h, 2 * k)
            else:
                sibling_send(p, h, 7)

    def columns_copy(d):
        b = lax.rem(column(y + d, zl), 3)
        return remote(
            up.at[:, pl.ds(pl.multiple_of(b * 256, 256), 256)], ub.at[zl, y, zh, c],
            a_snd.at[d], a_rcv.at[d], yc_id(d, 0),
        )

    def columns_own():
        b = lax.rem(column(y, zl), 3)
        return pltpu.make_async_copy(
            up.at[:, pl.ds(pl.multiple_of(b * 256, 256), 256)], ub.at[zl, y, zh, c], a_loc
        )

    held(0, 0, columns_own().start)
    for d in (1, 2, 3):
        pl.when(column(y + d, zl) < 3)(columns_copy(d).start)
    load[1].wait()

    me = y * 2 + c
    sbuf[me] = jnp.full((8, 128), strength[0], F32)
    others = [(d, b) for d in range(4) for b in range(2) if d or b]

    def strengths_copy(d, b):
        n = d * 2 + b
        return remote(sbuf.at[me], sbuf.at[me], s_snd.at[n], s_rcv.at[n], yc_id(d, b))

    for d, b in others:
        strengths_copy(d, b).start()

    rows = pl.ds(pl.multiple_of(c * 64, 64), 64)
    cols = pl.ds(pl.multiple_of(y * 1024, 1024), 1024)
    mine = pl.ds(pl.multiple_of(x * 64, 64), 64)
    pgb[mine, :] = (prompt[rows, :].astype(F32) * gain[...]).astype(BF16)

    def prompt_copy(d):
        return remote(pgb.at[mine, :], pgb.at[mine, :], p_snd.at[d], p_rcv.at[d], x_id(d))

    for d in (1, 2, 3):
        prompt_copy(d).start()
    steered = steer[...] * gain[...]
    high = steered.astype(BF16).astype(F32)
    which = lax.broadcasted_iota(jnp.int32, (16, D), 0)
    pgb[256:272, :] = jnp.where(which == 0, high, jnp.where(which == 1, steered - high, 0.0)).astype(BF16)

    load[2].wait()
    for p in (1, 2):
        for h in (0, 1):
            sibling_send(p, h, 0)
    held(0, 0, columns_own().wait)
    for d in (1, 2, 3):
        held(0, 0, columns_copy(d).wait_recv)
    ring_send(0, 0, 1)
    for h in (0, 1):
        sibling_send(0, h, 0)

    for d, b in others:
        strengths_copy(d, b).wait()
    lane = lax.broadcasted_iota(jnp.int32, (64, 128), 1)
    table = jnp.zeros((64, 128), F32)
    by_row[0] = jnp.transpose(ids[...].astype(F32))
    by_row[1] = jnp.transpose(gates[...])
    name = by_row[0, rows, :].astype(jnp.int32)
    weight = by_row[1, rows, :]
    for k in range(8):
        table = table + jnp.where(lane == name[:, k:k + 1], weight[:, k:k + 1], 0.0)
    misc[x] = table

    @pl.loop(0, 8)
    def _(j):
        s = sbuf[j][0:1, 0:1]
        square = jnp.zeros((64, 128), F32)
        for n in range(32):
            here = slice(n * 128, (n + 1) * 128)
            piece = prompt[rows, here].astype(F32) + s * steer[:, here]
            square = square + piece * piece
        mean = jnp.sum(square, axis=1, keepdims=True) * (1.0 / D)
        misc[x] = misc[x] + jnp.where(lane == 16 + j, lax.rsqrt(mean + epsilon), 0.0)

    def misc_copy(d):
        return remote(misc.at[x], misc.at[x], m_snd.at[d], m_rcv.at[d], x_id(d))

    for d in (1, 2, 3):
        misc_copy(d).start()
    for way in (0, 1):
        held(0, 0, ring(0, 0, way, 1).wait_send)
    ring_send(0, 1, 1)
    ring_take(0, 1)
    for h in (0, 1):
        ring_send(1, h, 1)

    def turn(i):
        return lax.rem(zl + TURN[i], 4)

    def expert(i):
        e = turn(i)
        b = column(y, e)

        @pl.when(b < 3)
        def _():
            for n in ((3, 4), (2, 5), (1, 6), (0, 7))[i]:
                for h in (0, 1):
                    sibling(0, h, n).wait_recv()
            upper = jnp.dot(pgb[...], ub[e].reshape(D, 256), preferred_element_type=F32)
            here = pl.ds(pl.multiple_of(b * 256, 256), 256)
            for block in range(4):
                ab[block, e, :, here] = upper[block * 64:(block + 1) * 64].astype(BF16)
            qb[y, e] = upper[256:257] + upper[257:258] + jnp.zeros((8, 256), F32)
            for d in (1, 3):
                gather_copy(i, d).start()
            for d in (1, 2, 3):
                push_copy(i, d).start()

    def owner(d):
        return y + (0 if d in (1, 3) else 3 if d == 2 else 1)

    def gather_copy(i, d):
        e = turn(i)
        here = pl.ds(pl.multiple_of(lax.rem(column(owner(d), e), 3) * 256, 256), 256)
        blocks = pl.ds(0, 4) if d in (1, 3) else pl.ds(0, 2) if d == 2 else pl.ds(2, 2)
        piece = ab.at[blocks, e, :, here]
        return remote(piece, piece, ag_snd.at[i, d], ag_rcv.at[i, d], yc_id((3, 1, 1, 3)[d], 0))

    def sent(i, d, fn):
        pl.when(column(owner(d), turn(i)) < 3)(fn)

    def came(i, d, fn):
        pl.when(column(y + (2, 3, 2, 1)[d], turn(i)) < 3)(fn)

    def forward(i):
        came(i, 1, gather_copy(i, 1).wait_recv)
        sent(i, 2, gather_copy(i, 2).start)
        came(i, 3, gather_copy(i, 3).wait_recv)
        sent(i, 0, gather_copy(i, 0).start)

    def push_copy(i, d):
        piece = qb.at[y, turn(i)]
        return remote(piece, piece, q_snd.at[i, d], q_rcv.at[i, d], yc_id(d, 0))

    for d in (1, 2, 3):
        misc_copy(d).wait_recv()

    @pl.loop(0, 4)
    def _(block):
        here = misc[block]
        for e in range(4):
            column = jnp.sum(jnp.where(lane == e * 4 + x, here, 0.0), axis=1, keepdims=True)
            gt[block, e] = jnp.broadcast_to(column, (64, 128))
        for j in range(8):
            it[block, j] = jnp.broadcast_to(0.5 * here[:, 16 + j:17 + j], (64, 128))

    def gathered(i):
        e = turn(i)
        for d in (0, 2):
            came(i, d, gather_copy(i, d).wait_recv)
        for d in (1, 2, 3):
            pl.when(column(y + 4 - d, e) < 3)(push_copy(i, d).wait_recv)
        for b in range(3):
            push = qb[lax.rem(e + b, 4), e]
            for j in range(8):
                sq[j, e, :, b * 256:(b + 1) * 256] = push * sbuf[j][:, 0:1]

        @pl.loop(0, 16)
        def _(n):
            block, g = n // 4, lax.rem(n, 4)
            gate = gt[block, e]
            for b in range(2):
                j = lax.rem(y + g + 1, 4) * 2 + b
                inv = it[block, j]
                for m in range(6):
                    here = slice(m * 128, (m + 1) * 128)
                    pre = ab[block, e, :, here].astype(F32).reshape(8, 8, 128) + sq[j, e, :, here][None]
                    half = pre.reshape(64, 128) * inv
                    value = (half * gate) * (1.0 + jnp.tanh(half))
                    hb[g, pl.ds(pl.multiple_of(block * 128 + b * 64, 64), 64),
                       pl.ds(pl.multiple_of(e * EH + m * 128, 128), 128)] = value.astype(BF16)

    ring_take(0, 2)
    ring_take(1, 1)
    for d in (1, 2, 3):
        prompt_copy(d).wait_recv()
    expert(0)
    ring_take(0, 3)
    ring_take(1, 2)
    expert(1)
    expert(2)
    forward(0)
    ring_take(0, 4)
    expert(3)
    ring_take(1, 3)
    for h in (0, 1):
        ring_send(2, h, 1)
    forward(1)
    forward(2)
    gathered(0)
    forward(3)
    ring_take(1, 4)
    gathered(1)
    ring_take(2, 1)
    gathered(2)
    gathered(3)

    def passed(p):
        for h in (0, 1):
            for n in range(8):
                sibling(p, h, n).wait_recv()

    def relay(u, way):
        return remote(
            rsend.at[u, way], rrecv.at[u, way], rl_snd.at[u, way], rl_rcv.at[u, way], x_id(1 + 2 * way)
        )

    def main(u, way):
        return remote(
            msend.at[u, way], mrecv.at[u, way], mn_snd.at[u, way], mn_rcv.at[u, way], x_id(1 + 2 * way)
        )

    def final(g, b):
        return remote(
            fin.at[g, pl.ds(pl.multiple_of(lax.rem(c + b, 2) * 64, 64), 64), :],
            out.at[0, rows, cols], f_snd.at[g, b], f_rcv.at[g, b], yc_id(g + 1, b),
        )

    def final_local():
        return pltpu.make_async_copy(fin.at[3, rows, :], out.at[0, rows, cols], f_loc)

    def multiply(u, half):
        g = lax.rem(u, 4)

        @pl.loop(0, 2)
        def _(way):
            sums = jnp.dot(hb[g], db[half, way], preferred_element_type=F32)
            place = pl.ds(pl.multiple_of(way * 256, 256), 256)
            for block in range(4):
                part[u, block, :, place] = sums[block * 128:(block + 1) * 128]
            rsend[u, way] = part[u, lax.rem(x + 2, 4), :, place].astype(BF16)
            relay(u, way).start()

    def pass_on(u):
        for way in (0, 1):
            relay(u, way).wait_recv()
            block = lax.rem(x + 1 + 2 * way, 4)
            same = slice(way * 256, way * 256 + 256)
            other = slice(256 - way * 256, 512 - way * 256)
            msend[u, way, :, same] = (part[u, block, :, same] + rrecv[u, way].astype(F32)).astype(BF16)
            msend[u, way, :, other] = part[u, block, :, other].astype(BF16)
            main(u, way).start()

    def finish(u, half):
        g = lax.rem(u, 4)
        main(u, 0).wait_recv()
        main(u, 1).wait_recv()
        for n in range(4):
            here = slice(n * 128, n * 128 + 128)
            fin[g, :, n * 256 + half * 128:n * 256 + half * 128 + 128] = (
                part[u, x, :, here] + mrecv[u, 0, :, here].astype(F32) + mrecv[u, 1, :, here].astype(F32)
            ).astype(BF16)

    passed(1)
    multiply(0, 0)
    ring_take(2, 2)
    multiply(1, 0)
    pass_on(0)
    ring_take(2, 3)
    multiply(2, 0)
    pass_on(1)
    finish(0, 0)
    ring_take(2, 4)
    multiply(3, 0)
    pass_on(2)
    finish(1, 0)

    passed(2)

    @pl.loop(4, 10)
    def _(t):
        @pl.when(t < 8)
        def _():
            multiply(t, 1)

        @pl.when(t < 9)
        def _():
            pass_on(t - 1)

        @pl.when(t < 6)
        def _():
            finish(t - 2, 0)

        @pl.when(t >= 6)
        def _():
            finish(t - 2, 1)
            g = t - 6
            final(g, 1).start()

            @pl.when(g < 3)
            def _():
                final(g, 0).start()

            @pl.when(g == 3)
            def _():
                final_local().start()

    for d in (1, 2, 3):
        prompt_copy(d).wait_send()
        misc_copy(d).wait_send()
        pl.when(column(y + d, zl) < 3)(columns_copy(d).wait_send)
    for i in range(4):
        for d in (1, 2, 3):
            sent(i, 1, push_copy(i, d).wait_send)
        for d in range(4):
            sent(i, d, gather_copy(i, d).wait_send)
    for p in range(3):
        for h in (0, 1):
            for k in (1, 2, 3, 4):
                for way in ways(h, k):
                    if (p, h, k) != (0, 0, 1):
                        held(p, (k - 1) * (2 * way - 1), ring(p, h, way, k).wait_send)
            for n in range(8):
                held(p, sibling_step(n), sibling(p, h, n).wait_send)
    for u in range(8):
        for way in (0, 1):
            relay(u, way).wait_send()
            main(u, way).wait_send()
    for g in range(4):
        for b in (0, 1):
            if (g, b) != (3, 0):
                final(g, b).wait()
    final_local().wait()


def local(prompt, steer_vec, strengths, norm_gain, expert_ids, gate_values, up_weight, down_weight):
    vmem = pl.BlockSpec(memory_space=pltpu.VMEM)
    away = pl.BlockSpec(memory_space=pl.ANY)
    dma = pltpu.SemaphoreType.DMA
    return pl.pallas_call(
        kernel,
        out_shape=jax.ShapeDtypeStruct((1, 128, D), BF16),
        in_specs=[vmem, vmem, pl.BlockSpec(memory_space=pltpu.SMEM)] + [vmem] * 4 + [away],
        out_specs=away,
        scratch_shapes=[
            pltpu.VMEM((8, 8, 128), F32),
            pltpu.VMEM((2, 128, 8), F32),
            pltpu.VMEM((272, D), BF16),
            pltpu.VMEM((4, 64, 128), F32),
            pltpu.VMEM((4, 4, 64, 128), F32),
            pltpu.VMEM((4, 8, 64, 128), F32),
            pltpu.VMEM((8, 4, 8, EH), F32),
            pltpu.VMEM((4, 4, 2, 2, 256, 256), BF16),
            pltpu.VMEM((2, 2, 4 * EH, 256), BF16),
            pltpu.VMEM((4, 4, 64, EH), BF16),
            pltpu.VMEM((4, 4, 8, 256), F32),
            pltpu.VMEM((4, 512, 4 * EH), BF16),
            pltpu.VMEM((8, 4, 128, 512), F32),
            pltpu.VMEM((8, 2, 128, 256), BF16),
            pltpu.VMEM((8, 2, 128, 256), BF16),
            pltpu.VMEM((8, 2, 128, 512), BF16),
            pltpu.VMEM((8, 2, 128, 512), BF16),
            pltpu.VMEM((4, 128, 1024), BF16),
            dma((3,)),
            dma((8,)), dma((8,)),
            dma((4,)), dma((4,)),
            dma((4,)), dma((4,)),
            dma((3, 2, 2, 4)), dma((3, 2, 2, 4)),
            dma((3, 2, 8)), dma((3, 2, 8)),
            dma((4,)), dma((4,)), dma(()),
            dma((4, 4)), dma((4, 4)),
            dma((4, 4)), dma((4, 4)),
            dma((8, 2)), dma((8, 2)),
            dma((8, 2)), dma((8, 2)),
            dma((4, 2)), dma((4, 2)),
            dma(()),
        ],
        compiler_params=pltpu.CompilerParams(
            collective_id=0, has_side_effects=True, vmem_limit_bytes=60 * 1024 * 1024
        ),
        cost_estimate=pl.CostEstimate(flops=18_000_000_000, bytes_accessed=3_000_000, transcendentals=6_300_000),
    )(
        prompt,
        steer_vec[None],
        strengths,
        norm_gain[None],
        expert_ids.T,
        gate_values.T,
        up_weight[0],
        down_weight[0],
    )


def solution(mesh):
    fine = Mesh(mesh.devices.reshape(4, 2, 2, 4, 4), ("y", "zh", "c", "zl", "x"))
    return jax.shard_map(
        local,
        mesh=fine,
        in_specs=(
            P(EXPERT, None),
            P(),
            P(WIDE),
            P(),
            P(EXPERT, None),
            P(EXPERT, None),
            P(EXPERT, WIDE, None),
            P(EXPERT, None, WIDE),
        ),
        out_specs=P(WIDE, EXPERT, None),
        check_vma=False,
    )
```
